32 devices in a mesh: leaf: 8 (over z, y), sub: 4 (over x, core).
Axes of the slice: x: 2, y: 2, z: 4, core: 2. Of those that a mesh axis runs over, the one named last changes fastest.
Arguments:
- fine_mult: bfloat16 [4096, 152], P(('leaf', 'sub')), may hold values from -6 to 6
- m2m_ops: bfloat16 [8, 152, 152], replicated, may hold values from -0.15625 to 0.15625
- m2l_ops: bfloat16 [316, 152, 152], replicated, may hold values from -0.03125 to 0.03125
- check_to_equiv: float32 [152, 152], replicated, may hold values from -0.5 to 0.5
- l2l_ops: bfloat16 [8, 152, 152], replicated, may hold values from -0.5 to 0.5
- send_slots: int32 [32, 32, 64], P(('leaf', 'sub')), may hold values from 0 to 127
- fine_list: int32 [4096, 189], P(('leaf', 'sub')), may hold values from 0 to 2175, as said below
- fine_class: int32 [4096, 189], P(('leaf', 'sub')), may hold values from 0 to 315
- fine_count: int32 [4096], P(('leaf', 'sub')), may hold values from 94 to 189, as said below
- parent_list: int32 [512, 189], P(('leaf', 'sub')), may hold values from 0 to 63
- parent_class: int32 [512, 189], P(('leaf', 'sub')), may hold values from 0 to 315
- parent_count: int32 [512], P(('leaf', 'sub')), may hold values from 94 to 189, as said below
Outputs:
- fine_local: float32 [4096, 152], P(('leaf', 'sub'))
The draws below stay inside these ranges and needn't reach their ends.
Inputs may be any that keep to these rules, and one draw needn't show every extreme that they name: `fine_list`: codes below 128 name a cell of the target's own device; larger codes name a slot of what another device sends to it. `fine_count`: some cell of every device has a full list. `parent_count`: some parent of every device has a full list.
All inputs are finite; a program needn't handle non-finite values.
Results may differ from the reference program's by a relative error of at most 0.0026.
Values may be sent and summed in bfloat16 or wider, within the bound.
A program may use at most 128 MiB of HBM per device.

```python
import math
import jax
import jax.numpy as jnp
from jax import lax

Q = 152
CLS = 316
LIST = 189
C_DEV = 128
CAP = 64
PARENTS_DEV = 16
PEERS = 32
CELLS = 4096
PARENTS = 512
BLOCK_PARENTS = 64


def draw_fine_list(key, part):
    key = jax.random.fold_in(key, 11)
    first_key, second_key, third_key = jax.random.split(key, 3)
    local_code = jax.random.randint(first_key, (CELLS, LIST), 0, C_DEV)
    remote_code = C_DEV + jax.random.randint(second_key, (CELLS, LIST), 0, PEERS * CAP)
    pick_local = jax.random.randint(third_key, (CELLS, LIST), 0, 2) == 0
    codes = jnp.where(pick_local, local_code, remote_code)
    codes = codes.at[0, LIST - 1].set(C_DEV + PEERS * CAP - 1)
    codes = codes.at[0, 0].set(0)
    return codes.astype(jnp.int32)


def draw_fine_count(key, part):
    key = jax.random.fold_in(key, 12)
    base = jax.random.randint(key, (CELLS,), LIST // 2, LIST + 1)
    position = jnp.arange(CELLS) % C_DEV
    base = jnp.where(position == 0, LIST, jnp.where(position == 1, LIST // 2, base))
    return base.astype(jnp.int32)


def draw_parent_count(key, part):
    key = jax.random.fold_in(key, 13)
    base = jax.random.randint(key, (PARENTS,), LIST // 2, LIST + 1)
    position = jnp.arange(PARENTS) % PARENTS_DEV
    device_even = jnp.arange(PARENTS) // PARENTS_DEV % 2 == 0
    base = jnp.where(position == 0, LIST, jnp.where((position == 1) & device_even, LIST // 2, base))
    return base.astype(jnp.int32)


def set_ends(entries, stream_key, smallest, top_value):
    longest = entries.shape.index(max(entries.shape))
    spots = []
    for shift in (0, 1):
        where = [jax.random.randint(jax.random.fold_in(stream_key, axis), (), 0, length) for axis, length in enumerate(entries.shape)]
        where[longest] = (where[longest] + shift) % entries.shape[longest]
        spots.append(tuple(where))
    return entries.at[spots[0]].set(smallest).at[spots[1]].set(top_value)


def block_levels(stream_key, extent, cuts, low, high):
    def one(axis_at, blocks):
        steps = jax.random.uniform(jax.random.fold_in(jax.random.fold_in(stream_key, 6), axis_at), (blocks,), jnp.float32, low / len(cuts), high / len(cuts))
        return jnp.repeat(jnp.exp(steps), extent[axis_at] // blocks).reshape((-1,) + (1,) * (len(extent) - axis_at - 1))

    loudness = one(*cuts[0])
    for cut in cuts[1:]:
        loudness = loudness * one(*cut)
    return loudness


def bell_draw(rng, dims, spread, reach, cuts=(), kind=jnp.bfloat16):
    result = spread * jax.random.normal(rng, dims, jnp.float32)
    if cuts:
        result = result * block_levels(rng, dims, cuts, -0.22, 0.18)
    return jnp.clip(result, -reach, reach).astype(kind)


def setup_inputs(seed: int = 0) -> dict:
    seeds = jax.random.split(jax.random.key(seed), 13)
    return {
        "fine_mult": bell_draw(seeds[0], (CELLS, Q), 1.0, 6.0, ((0, 32),)),
        "m2m_ops": bell_draw(seeds[1], (8, Q, Q), (8 * Q) ** -0.5, 0.15625),
        "m2l_ops": bell_draw(seeds[2], (CLS, Q, Q), (Q * LIST) ** -0.5, 0.03125),
        "check_to_equiv": bell_draw(seeds[3], (Q, Q), Q ** -0.5, 0.5, (), jnp.float32),
        "l2l_ops": bell_draw(seeds[4], (8, Q, Q), Q ** -0.5, 0.5),
        "send_slots": set_ends(jax.random.randint(seeds[5], (PEERS, PEERS, CAP), 0, C_DEV), jax.random.fold_in(seeds[5], 1), 0, C_DEV - 1).astype(jnp.int32),
        "fine_list": draw_fine_list(jax.random.fold_in(seeds[12], 71), 0),
        "fine_class": set_ends(jax.random.randint(seeds[7], (CELLS, LIST), 0, CLS), jax.random.fold_in(seeds[7], 1), 0, CLS - 1).astype(jnp.int32),
        "fine_count": draw_fine_count(jax.random.fold_in(seeds[12], 71), 0),
        "parent_list": set_ends(jax.random.randint(seeds[9], (PARENTS, LIST), 0, BLOCK_PARENTS), jax.random.fold_in(seeds[9], 1), 0, BLOCK_PARENTS - 1).astype(jnp.int32),
        "parent_class": set_ends(jax.random.randint(seeds[10], (PARENTS, LIST), 0, CLS), jax.random.fold_in(seeds[10], 1), 0, CLS - 1).astype(jnp.int32),
        "parent_count": draw_parent_count(jax.random.fold_in(seeds[12], 71), 0),
    }


def translate(source_table, global_source, entry_class, entry_count, m2l_ops):
    targets, slot_count = global_source.shape
    classes, points, _ = m2l_ops.shape
    block_size = math.gcd(targets, 512)
    flat_ops = m2l_ops.reshape(classes * points, points)

    def translate_block(pieces):
        chosen, kinds, lengths = pieces
        gathered = jnp.take(source_table, chosen.reshape(-1), axis=0).astype(jnp.float32)
        active_slot = lax.broadcasted_iota(jnp.int32, chosen.shape, 1) < lengths[:, None]
        gathered = gathered * active_slot.reshape(-1, 1).astype(jnp.float32)
        segment = lax.broadcasted_iota(jnp.int32, chosen.shape, 0) * classes + kinds
        summed = jax.ops.segment_sum(gathered, segment.reshape(-1), num_segments=block_size * classes)
        summed = summed.astype(jnp.bfloat16).reshape(block_size, classes * points)
        return jnp.dot(summed, flat_ops, preferred_element_type=jnp.float32)

    results = lax.map(translate_block, (global_source.reshape(-1, block_size, slot_count),
                                        entry_class.reshape(-1, block_size, slot_count),
                                        entry_count.reshape(-1, block_size)))
    return results.reshape(targets, points)


def reference(fine_mult, m2m_ops, m2l_ops, check_to_equiv, l2l_ops, send_slots, fine_list, fine_class,
              fine_count, parent_list, parent_class, parent_count):
    cell_total, points = fine_mult.shape
    device_of = (jnp.arange(cell_total, dtype=jnp.int32) // C_DEV)[:, None]
    remote = jnp.maximum(fine_list - C_DEV, 0)
    source_device = remote // CAP
    source_slot = remote % CAP
    remote_cell = send_slots[source_device, jnp.broadcast_to(device_of, fine_list.shape), source_slot]
    global_source = jnp.where(fine_list < C_DEV, device_of * C_DEV + fine_list,
                              source_device * C_DEV + remote_cell).astype(jnp.int32)
    fine_check = translate(fine_mult, global_source, fine_class, fine_count, m2l_ops)
    children = fine_mult.reshape(cell_total // 8, 8, points).astype(jnp.float32)
    parent_mult = jnp.einsum('pkq,kqr->pr', children, m2m_ops.astype(jnp.float32)).astype(jnp.bfloat16)
    parent_total = parent_mult.shape[0]
    block_start = (jnp.arange(parent_total, dtype=jnp.int32) // BLOCK_PARENTS * BLOCK_PARENTS)[:, None]
    parent_source = (block_start + parent_list).astype(jnp.int32)
    parent_check = 0.5 * translate(parent_mult, parent_source, parent_class, parent_count, m2l_ops)
    parent_local = jnp.dot(parent_check, check_to_equiv, precision=lax.Precision.HIGHEST,
                           preferred_element_type=jnp.float32).astype(jnp.bfloat16)
    downward = jnp.einsum('pq,kqr->pkr', parent_local.astype(jnp.float32), l2l_ops.astype(jnp.float32))
    return fine_check + downward.reshape(cell_total, points)
```

```python
import functools

import jax
import jax.numpy as jnp
from jax import lax
from jax.experimental import pallas as pl
from jax.experimental.pallas import tpu as pltpu
from jax.sharding import PartitionSpec as P

GROUP = 16
CHUNK = 4
BUFFERS = 8


def translate_kernel(targets, slots, classes, points, row_ref, sum_ref, steps_ref, table_ref, ops_ref, out_ref,
                     sums, ops, sems):
    chunks = classes // CHUNK

    def fetch(chunk, buffer):
        return pltpu.make_async_copy(ops_ref.at[pl.ds(chunk * CHUNK, CHUNK)], ops.at[buffer], sems.at[buffer])

    for b in range(BUFFERS):
        fetch(b, b).start()

    flat = sums.reshape(sums.shape[0] * 2, 128)

    def clear(i, _):
        flat[pl.ds(i * 2 * targets, 2 * targets), :] = jnp.zeros((2 * targets, 128), jnp.float32)
        return 0

    lax.fori_loop(0, classes, clear, 0)

    def group(g, _):
        def step(e, _):
            base = (g * slots + e) * GROUP
            places = [sum_ref[base + i] for i in range(GROUP)]
            rows = [row_ref[base + i] for i in range(GROUP)]
            values = [sums[places[i]] + table_ref[rows[i]] for i in range(GROUP)]
            for i in range(GROUP):
                sums[places[i]] = values[i]
            return 0

        lax.fori_loop(0, steps_ref[g], step, 0)
        return 0

    lax.fori_loop(0, targets // GROUP, group, 0)

    out_ref[...] = jnp.zeros_like(out_ref)

    def multiply(chunk, _):
        buffer = lax.rem(chunk, BUFFERS)
        fetch(chunk, buffer).wait()
        total = out_ref[...]
        for i in range(CHUNK):
            start = (chunk * CHUNK + i) * 2 * targets
            low = flat[pl.ds(start, targets, stride=2), :]
            high = flat[pl.ds(start + 1, targets, stride=2), :]
            left = jnp.concatenate([low.astype(jnp.bfloat16), high.astype(jnp.bfloat16)], axis=1)[:, :points]
            total += jnp.dot(left, ops[buffer, i], preferred_element_type=jnp.float32)
        out_ref[...] = total

        @pl.when(chunk + BUFFERS < chunks)
        def _():
            fetch(chunk + BUFFERS, buffer).start()

        return 0

    lax.fori_loop(0, chunks, multiply, 0)


def translate(table, entry_row, entry_class, entry_count, m2l_ops):
    targets, slots = entry_row.shape
    classes, points, _ = m2l_ops.shape
    groups = targets // GROUP
    live = lax.broadcasted_iota(jnp.int32, entry_row.shape, 1) < entry_count[:, None]
    target = lax.broadcasted_iota(jnp.int32, entry_row.shape, 0)
    places = jnp.where(live, entry_class, classes) * targets + target

    def arrange(x):
        return x.reshape(groups, GROUP, slots).transpose(0, 2, 1).reshape(-1)

    steps = jnp.max(entry_count.reshape(groups, GROUP), axis=1)
    smem = pl.BlockSpec(memory_space=pltpu.SMEM)
    vmem = pl.BlockSpec(memory_space=pltpu.VMEM)
    return pl.pallas_call(
        functools.partial(translate_kernel, targets, slots, classes, points),
        out_shape=jax.ShapeDtypeStruct((targets, points), jnp.float32),
        in_specs=[smem, smem, smem, vmem, pl.BlockSpec(memory_space=pl.ANY)],
        out_specs=vmem,
        scratch_shapes=[
            pltpu.VMEM(((classes + 1) * targets, 2, 128), jnp.float32),
            pltpu.VMEM((BUFFERS, CHUNK, points, points), jnp.bfloat16),
            pltpu.SemaphoreType.DMA((BUFFERS,)),
        ],
        compiler_params=pltpu.CompilerParams(vmem_limit_bytes=62 * 2**20),
    )(arrange(entry_row), arrange(places), steps, table, m2l_ops)


def body(
    fine_mult,
    m2m_ops,
    m2l_ops,
    check_to_equiv,
    l2l_ops,
    send_slots,
    fine_list,
    fine_class,
    fine_count,
    parent_list,
    parent_class,
    parent_count,
):
    cell_total, points = fine_mult.shape
    peer_count = send_slots.shape[1]
    capacity = send_slots.shape[2]
    outgoing = jnp.take(fine_mult, send_slots[0].reshape(-1), axis=0, mode="clip")
    outgoing = outgoing.reshape(peer_count, capacity, points)
    received = lax.all_to_all(outgoing, ("leaf", "sub"), split_axis=0, concat_axis=0, tiled=True)
    received = received.reshape(peer_count * capacity, points)
    children = fine_mult.reshape(cell_total // 8, 8, points)
    parent_mult = jnp.einsum(
        "pkq,kqr->pr", children, m2m_ops, preferred_element_type=jnp.float32
    ).astype(jnp.bfloat16)
    block_parents = lax.all_gather(parent_mult, "sub", axis=0, tiled=True)
    table = jnp.concatenate([fine_mult, received, block_parents], axis=0).astype(jnp.float32)
    table = jnp.pad(table, ((0, 0), (0, 256 - points))).reshape(-1, 2, 128)
    parent_first = cell_total + peer_count * capacity
    check = translate(
        table,
        jnp.concatenate([fine_list, parent_list + parent_first], axis=0),
        jnp.concatenate([fine_class, parent_class], axis=0),
        jnp.concatenate([fine_count, parent_count], axis=0),
        m2l_ops,
    )
    fine_check, parent_check = check[:cell_total], 0.5 * check[cell_total:]
    parent_local = jnp.dot(
        parent_check,
        check_to_equiv,
        precision=lax.Precision.HIGHEST,
        preferred_element_type=jnp.float32,
    ).astype(jnp.bfloat16)
    downward = jnp.einsum("pq,kqr->pkr", parent_local, l2l_ops, preferred_element_type=jnp.float32)
    return fine_check + downward.reshape(cell_total, points)


def solution(mesh):
    in_specs = (
        P(("leaf", "sub"), None),
        P(),
        P(),
        P(),
        P(),
        P(("leaf", "sub"), None, None),
        P(("leaf", "sub"), None),
        P(("leaf", "sub"), None),
        P(("leaf", "sub")),
        P(("leaf", "sub"), None),
        P(("leaf", "sub"), None),
        P(("leaf", "sub")),
    )
    out_specs = P(("leaf", "sub"), None)
    return jax.shard_map(body, mesh=mesh, in_specs=in_specs, out_specs=out_specs, check_vma=False)
```

```python
import functools

import jax
import jax.numpy as jnp
from jax import lax
from jax.experimental import pallas as pl
from jax.experimental.pallas import tpu as pltpu
from jax.sharding import PartitionSpec as P

PARTS = 4


def translate_kernel(targets, slots, classes, points, row_ref, kind_ref, table_ref, ops_ref, out_ref, sums, ops,
                     even, odd, sems):
    part = points // PARTS
    columns = -(-classes // 128) * 128
    depth = even.shape[0]

    def fetch(p):
        piece = pl.ds(p * part, part)
        return pltpu.make_async_copy(ops_ref.at[piece], ops.at[piece], sems.at[p])

    for p in range(PARTS):
        fetch(p).start()

    def gather(t, chosen):
        for e in range(slots):
            chosen[e] = table_ref[row_ref[e * targets + t]]

    def sum_classes(t, chosen):
        flat = chosen.reshape(2 * depth, 128)
        low = flat[pl.ds(0, depth, stride=2), :].T
        high = flat[pl.ds(1, depth, stride=2), :].T
        left = jnp.concatenate([low, high[: points - 128]], axis=0).astype(jnp.bfloat16)
        kinds = kind_ref[pl.ds(t, 1), :]
        wanted = lax.broadcasted_iota(jnp.int32, (columns, depth), 0)
        onehot = jnp.where(kinds == wanted, 1.0, 0.0).astype(jnp.bfloat16)
        total = lax.dot_general(left, onehot, (((1,), (1,)), ((), ())), preferred_element_type=jnp.float32)
        for l in range(columns // 128):
            sums[pl.ds(l * points * targets + t, points, stride=targets), :] = total[:, 128 * l: 128 * l + 128]

    for chosen in (even, odd):
        chosen[pl.ds(slots, depth - slots)] = jnp.zeros((depth - slots, 2, 128), jnp.float32)
    gather(0, even)

    def pair(h, _):
        t = 2 * h
        gather(t + 1, odd)
        sum_classes(t, even)
        gather(lax.min(t + 2, targets - 1), even)
        sum_classes(t + 1, odd)
        return 0

    lax.fori_loop(0, targets // 2, pair, 0)

    for p in range(PARTS):
        fetch(p).wait()

    def multiply(i, total):
        left = jnp.concatenate(
            [sums[pl.ds(pl.multiple_of((l * points + i) * targets, 8), targets), :].astype(jnp.bfloat16)
             for l in range(columns // 128)], axis=1)[:, :classes]
        return total + lax.dot_general(left, ops[i], (((1,), (1,)), ((), ())), preferred_element_type=jnp.float32)

    out_ref[...] = lax.fori_loop(0, points, multiply, jnp.zeros((targets, points), jnp.float32), unroll=4)


def translate(table, entry_row, entry_class, entry_count, m2l_ops):
    targets, slots = entry_row.shape
    classes, points, _ = m2l_ops.shape
    depth = -(-slots // 64) * 64
    columns = -(-classes // 128) * 128
    live = lax.broadcasted_iota(jnp.int32, entry_row.shape, 1) < entry_count[:, None]
    kinds = jnp.pad(jnp.where(live, entry_class, -1), ((0, 0), (0, depth - slots)), constant_values=-1)
    smem = pl.BlockSpec(memory_space=pltpu.SMEM)
    vmem = pl.BlockSpec(memory_space=pltpu.VMEM)
    return pl.pallas_call(
        functools.partial(translate_kernel, targets, slots, classes, points),
        out_shape=jax.ShapeDtypeStruct((targets, points), jnp.float32),
        in_specs=[smem, vmem, vmem, pl.BlockSpec(memory_space=pl.ANY)],
        out_specs=vmem,
        scratch_shapes=[
            pltpu.VMEM((columns // 128 * points * targets, 128), jnp.float32),
            pltpu.VMEM((points, points, classes), jnp.bfloat16),
            pltpu.VMEM((depth, 2, 128), jnp.float32),
            pltpu.VMEM((depth, 2, 128), jnp.float32),
            pltpu.SemaphoreType.DMA((PARTS,)),
        ],
        compiler_params=pltpu.CompilerParams(vmem_limit_bytes=62 * 2**20),
    )(entry_row.T.reshape(-1), kinds, table, m2l_ops.transpose(1, 2, 0))


def body(
    fine_mult,
    m2m_ops,
    m2l_ops,
    check_to_equiv,
    l2l_ops,
    send_slots,
    fine_list,
    fine_class,
    fine_count,
    parent_list,
    parent_class,
    parent_count,
):
    cell_total, points = fine_mult.shape
    peer_count = send_slots.shape[1]
    capacity = send_slots.shape[2]
    wanted = lax.broadcasted_iota(jnp.int32, (1, cell_total), 1)
    onehot = (send_slots[0].reshape(-1, 1) == wanted).astype(jnp.bfloat16)
    outgoing = jnp.dot(onehot, fine_mult, preferred_element_type=jnp.float32).astype(jnp.bfloat16)
    outgoing = outgoing.reshape(peer_count, capacity, points)
    received = lax.all_to_all(outgoing, ("leaf", "sub"), split_axis=0, concat_axis=0, tiled=True)
    received = received.reshape(peer_count * capacity, points)
    children = fine_mult.reshape(cell_total // 8, 8, points)
    parent_mult = jnp.einsum(
        "pkq,kqr->pr", children, m2m_ops, preferred_element_type=jnp.float32
    ).astype(jnp.bfloat16)
    block_parents = lax.all_gather(parent_mult, "sub", axis=0, tiled=True)
    table = jnp.concatenate([fine_mult, received, block_parents], axis=0).astype(jnp.float32)
    table = jnp.pad(table, ((0, 0), (0, 256 - points))).reshape(-1, 2, 128)
    parent_first = cell_total + peer_count * capacity
    check = translate(
        table,
        jnp.concatenate([fine_list, parent_list + parent_first], axis=0),
        jnp.concatenate([fine_class, parent_class], axis=0),
        jnp.concatenate([fine_count, parent_count], axis=0),
        m2l_ops,
    )
    fine_check, parent_check = check[:cell_total], 0.5 * check[cell_total:]
    parent_local = jnp.dot(
        parent_check,
        check_to_equiv,
        precision=lax.Precision.HIGHEST,
        preferred_element_type=jnp.float32,
    ).astype(jnp.bfloat16)
    downward = jnp.einsum("pq,kqr->pkr", parent_local, l2l_ops, preferred_element_type=jnp.float32)
    return fine_check + downward.reshape(cell_total, points)


def solution(mesh):
    in_specs = (
        P(("leaf", "sub"), None),
        P(),
        P(),
        P(),
        P(),
        P(("leaf", "sub"), None, None),
        P(("leaf", "sub"), None),
        P(("leaf", "sub"), None),
        P(("leaf", "sub")),
        P(("leaf", "sub"), None),
        P(("leaf", "sub"), None),
        P(("leaf", "sub")),
    )
    out_specs = P(("leaf", "sub"), None)
    return jax.shard_map(body, mesh=mesh, in_specs=in_specs, out_specs=out_specs, check_vma=False)
```

```python
import functools

import jax
import jax.numpy as jnp
from jax import lax
from jax.experimental import pallas as pl
from jax.experimental.pallas import tpu as pltpu
from jax.sharding import PartitionSpec as P

PARTS = 4
BATCH = 4
EXTRA = 1


def translate_kernel(targets, slots, classes, points, row_ref, kind_ref, table_ref, ops_ref, out_ref, sums, ops,
                     even, odd, sems):
    part = points // PARTS
    columns = -(-classes // 128) * 128
    depth = even.shape[0] // BATCH
    pitch = targets + EXTRA

    def fetch(p):
        piece = pl.ds(p * part, part)
        return pltpu.make_async_copy(ops_ref.at[piece], ops.at[piece], sems.at[p])

    for p in range(PARTS):
        fetch(p).start()

    def gather(t, u, chosen):
        for e in range(slots):
            chosen[u * depth + e] = table_ref[row_ref[e * targets + t]]

    def class_sums(t, u, chosen):
        flat = chosen.reshape(2 * BATCH * depth, 128)
        low = flat[pl.ds(2 * u * depth, depth, stride=2), :].astype(jnp.bfloat16)
        high = flat[pl.ds(2 * u * depth + 1, depth, stride=2), :].astype(jnp.bfloat16)
        left = jnp.concatenate([low, high], axis=1)[:, :points].T
        kinds = kind_ref[pl.ds(t, 1), :]
        wanted = lax.broadcasted_iota(jnp.int32, (columns, depth), 0)
        onehot = jnp.where(kinds == wanted, 1.0, 0.0).astype(jnp.bfloat16)
        return lax.dot_general(left, onehot, (((1,), (1,)), ((), ())), preferred_element_type=jnp.float32)

    def keep(t, total):
        for l in range(columns // 128):
            sums[pl.ds(l * points * pitch + t, points, stride=pitch), :] = total[:, 128 * l: 128 * l + 128]

    for chosen in (even, odd):
        for u in range(BATCH):
            chosen[pl.ds(u * depth + slots, depth - slots)] = jnp.zeros((depth - slots, 2, 128), jnp.float32)
    for u in range(BATCH):
        gather(u, u, even)

    def pair(h, _):
        first = 2 * BATCH * h
        for now, later in ((even, odd), (odd, even)):
            following = lax.min(first + BATCH, targets - BATCH)
            for u in range(BATCH):
                total = class_sums(first + u, u, now)
                gather(following + u, u, later)
                keep(first + u, total)
            first += BATCH
        return 0

    lax.fori_loop(0, targets // (2 * BATCH), pair, 0)

    for p in range(PARTS):
        fetch(p).wait()

    def multiply(i, total):
        left = jnp.concatenate(
            [sums[pl.ds((l * points + i) * pitch, targets), :].astype(jnp.bfloat16)
             for l in range(columns // 128)], axis=1)[:, :classes]
        return total + lax.dot_general(left, ops[i], (((1,), (1,)), ((), ())), preferred_element_type=jnp.float32)

    out_ref[...] = lax.fori_loop(0, points, multiply, jnp.zeros((targets, points), jnp.float32), unroll=4)


def translate(table, entry_row, entry_class, entry_count, m2l_ops):
    targets, slots = entry_row.shape
    classes, points, _ = m2l_ops.shape
    depth = -(-slots // 64) * 64
    columns = -(-classes // 128) * 128
    live = lax.broadcasted_iota(jnp.int32, entry_row.shape, 1) < entry_count[:, None]
    kinds = jnp.pad(jnp.where(live, entry_class, -1), ((0, 0), (0, depth - slots)), constant_values=-1)
    smem = pl.BlockSpec(memory_space=pltpu.SMEM)
    vmem = pl.BlockSpec(memory_space=pltpu.VMEM)
    return pl.pallas_call(
        functools.partial(translate_kernel, targets, slots, classes, points),
        out_shape=jax.ShapeDtypeStruct((targets, points), jnp.float32),
        in_specs=[smem, vmem, vmem, pl.BlockSpec(memory_space=pl.ANY)],
        out_specs=vmem,
        scratch_shapes=[
            pltpu.VMEM((columns // 128 * points * (targets + EXTRA), 128), jnp.float32),
            pltpu.VMEM((points, points, classes), jnp.bfloat16),
            pltpu.VMEM((BATCH * depth, 2, 128), jnp.float32),
            pltpu.VMEM((BATCH * depth, 2, 128), jnp.float32),
            pltpu.SemaphoreType.DMA((PARTS,)),
        ],
        compiler_params=pltpu.CompilerParams(vmem_limit_bytes=62 * 2**20),
    )(entry_row.T.reshape(-1), kinds, table, m2l_ops.transpose(1, 2, 0))


def body(
    fine_mult,
    m2m_ops,
    m2l_ops,
    check_to_equiv,
    l2l_ops,
    send_slots,
    fine_list,
    fine_class,
    fine_count,
    parent_list,
    parent_class,
    parent_count,
):
    cell_total, points = fine_mult.shape
    peer_count = send_slots.shape[1]
    capacity = send_slots.shape[2]
    wanted = lax.broadcasted_iota(jnp.int32, (1, cell_total), 1)
    onehot = (send_slots[0].reshape(-1, 1) == wanted).astype(jnp.bfloat16)
    outgoing = jnp.dot(onehot, fine_mult, preferred_element_type=jnp.float32).astype(jnp.bfloat16)
    outgoing = outgoing.reshape(peer_count, capacity, points)
    received = lax.all_to_all(outgoing, ("leaf", "sub"), split_axis=0, concat_axis=0, tiled=True)
    received = received.reshape(peer_count * capacity, points)
    children = fine_mult.reshape(cell_total // 8, 8, points)
    parent_mult = jnp.einsum(
        "pkq,kqr->pr", children, m2m_ops, preferred_element_type=jnp.float32
    ).astype(jnp.bfloat16)
    block_parents = lax.all_gather(parent_mult, "sub", axis=0, tiled=True)
    table = jnp.concatenate([fine_mult, received, block_parents], axis=0).astype(jnp.float32)
    table = jnp.pad(table, ((0, 0), (0, 256 - points))).reshape(-1, 2, 128)
    parent_first = cell_total + peer_count * capacity
    check = translate(
        table,
        jnp.concatenate([fine_list, parent_list + parent_first], axis=0),
        jnp.concatenate([fine_class, parent_class], axis=0),
        jnp.concatenate([fine_count, parent_count], axis=0),
        m2l_ops,
    )
    fine_check, parent_check = check[:cell_total], 0.5 * check[cell_total:]
    parent_local = jnp.dot(
        parent_check,
        check_to_equiv,
        precision=lax.Precision.HIGHEST,
        preferred_element_type=jnp.float32,
    ).astype(jnp.bfloat16)
    downward = jnp.einsum("pq,kqr->pkr", parent_local, l2l_ops, preferred_element_type=jnp.float32)
    return fine_check + downward.reshape(cell_total, points)


def solution(mesh):
    in_specs = (
        P(("leaf", "sub"), None),
        P(),
        P(),
        P(),
        P(),
        P(("leaf", "sub"), None, None),
        P(("leaf", "sub"), None),
        P(("leaf", "sub"), None),
        P(("leaf", "sub")),
        P(("leaf", "sub"), None),
        P(("leaf", "sub"), None),
        P(("leaf", "sub")),
    )
    out_specs = P(("leaf", "sub"), None)
    return jax.shard_map(body, mesh=mesh, in_specs=in_specs, out_specs=out_specs, check_vma=False)
```

```python
import functools

import jax
import jax.numpy as jnp
from jax import lax
from jax.experimental import pallas as pl
from jax.experimental.pallas import tpu as pltpu
from jax.sharding import PartitionSpec as P

PARTS = 4
FOLD = 4
BATCH = 4
EXTRA = 1


def exchange_kernel(peers, subs, out_ref, mine_ref, received_ref, parents_ref, send_sems, recv_sems, parent_send,
                    parent_recv, own_sems):
    leaf, sub = lax.axis_index("leaf"), lax.axis_index("sub")
    me = leaf * subs + sub
    barrier = pltpu.get_barrier_semaphore()

    def cells(o):
        other = lax.rem(me + o, peers)
        return pltpu.make_async_remote_copy(
            src_ref=out_ref.at[other], dst_ref=received_ref.at[me], send_sem=send_sems.at[o], recv_sem=recv_sems.at[o],
            device_id=(other // subs, lax.rem(other, subs)), device_id_type=pl.DeviceIdType.MESH)

    def parents(o):
        return pltpu.make_async_remote_copy(
            src_ref=mine_ref, dst_ref=parents_ref.at[sub], send_sem=parent_send.at[o], recv_sem=parent_recv.at[o],
            device_id=(leaf, lax.rem(sub + o, subs)), device_id_type=pl.DeviceIdType.MESH)

    def greet(o, _):
        other = lax.rem(me + o, peers)
        pl.semaphore_signal(barrier, inc=1, device_id=(other // subs, lax.rem(other, subs)),
                            device_id_type=pl.DeviceIdType.MESH)
        return 0

    lax.fori_loop(1, peers, greet, 0)
    own = pltpu.make_async_copy(out_ref.at[me], received_ref.at[me], own_sems.at[0])
    own_parents = pltpu.make_async_copy(mine_ref, parents_ref.at[sub], own_sems.at[1])
    own.start()
    own_parents.start()
    pl.semaphore_wait(barrier, peers - 1)

    def start(o, _):
        cells(o).start()
        return 0

    def finish(o, _):
        cells(o).wait()
        return 0

    lax.fori_loop(1, peers, start, 0)
    for o in range(1, subs):
        parents(o).start()
    own.wait()
    own_parents.wait()
    for o in range(1, subs):
        parents(o).wait()
    lax.fori_loop(1, peers, finish, 0)


def exchange(outgoing, mine, peers, subs):
    vmem = pl.BlockSpec(memory_space=pltpu.VMEM)
    return pl.pallas_call(
        functools.partial(exchange_kernel, peers, subs),
        out_shape=(jax.ShapeDtypeStruct(outgoing.shape, outgoing.dtype),
                   jax.ShapeDtypeStruct((subs,) + mine.shape, mine.dtype)),
        in_specs=[vmem, vmem],
        out_specs=(vmem, vmem),
        scratch_shapes=[
            pltpu.SemaphoreType.DMA((peers,)),
            pltpu.SemaphoreType.DMA((peers,)),
            pltpu.SemaphoreType.DMA((subs,)),
            pltpu.SemaphoreType.DMA((subs,)),
            pltpu.SemaphoreType.DMA((2,)),
        ],
        compiler_params=pltpu.CompilerParams(collective_id=0, has_side_effects=True, vmem_limit_bytes=16 * 2**20),
    )(outgoing, mine)


def translate_kernel(targets, slots, classes, points, row_ref, kind_ref, mult_ref, received_ref, parents_ref, ops_ref,
                     out_ref, table_ref, sums, ops, even, odd, sems):
    part = points // PARTS
    columns = -(-classes // 128) * 128
    depth = even.shape[0] // BATCH
    pitch = targets + EXTRA

    def fetch(p):
        piece = pl.ds(p * part, part)
        return pltpu.make_async_copy(ops_ref.at[piece], ops.at[piece], sems.at[p])

    for p in range(PARTS):
        fetch(p).start()

    cells = mult_ref.shape[0]
    peers, packed, _ = received_ref.shape
    subs, both, _ = parents_ref.shape
    capacity, own = packed * FOLD // (FOLD + 1), both // 2
    rest = points - 128
    rows = table_ref.reshape(table_ref.shape[0] * 2, 128)
    mult = mult_ref[...].astype(jnp.float32)
    rows[pl.ds(0, cells, stride=2), :] = mult[:, :128]
    rows[pl.ds(1, cells, stride=2), :] = jnp.concatenate(
        [mult[:, 128:], jnp.zeros((cells, 128 - rest), jnp.float32)], axis=1)

    def unpack(s, _):
        first = 2 * (cells + s * capacity)
        rows[pl.ds(first, capacity, stride=2), :] = received_ref[s, :capacity].astype(jnp.float32)
        high = received_ref[s, capacity:].astype(jnp.float32)
        for q in range(FOLD):
            rows[pl.ds(first + 2 * q * (capacity // FOLD) + 1, capacity // FOLD, stride=2), :] = (
                pltpu.roll(high, 128 - rest * q, 1) if q else high)
        return 0

    lax.fori_loop(0, peers, unpack, 0)
    for s in range(subs):
        first = 2 * (cells + peers * capacity + s * own)
        rows[pl.ds(first, own, stride=2), :] = parents_ref[s, :own].astype(jnp.float32)
        rows[pl.ds(first + 1, own, stride=2), :] = parents_ref[s, own:].astype(jnp.float32)

    def gather(t, u, chosen):
        for e in range(slots):
            chosen[u * depth + e] = table_ref[row_ref[e * targets + t]]

    def class_sums(t, u, chosen):
        flat = chosen.reshape(2 * BATCH * depth, 128)
        low = flat[pl.ds(2 * u * depth, depth, stride=2), :].astype(jnp.bfloat16)
        high = flat[pl.ds(2 * u * depth + 1, depth, stride=2), :].astype(jnp.bfloat16)
        left = jnp.concatenate([low, high], axis=1)[:, :points].T
        kinds = kind_ref[pl.ds(t, 1), :]
        wanted = lax.broadcasted_iota(jnp.int32, (columns, depth), 0)
        onehot = jnp.where(kinds == wanted, 1.0, 0.0).astype(jnp.bfloat16)
        return lax.dot_general(left, onehot, (((1,), (1,)), ((), ())), preferred_element_type=jnp.float32)

    def keep(t, total):
        for l in range(columns // 128):
            sums[pl.ds(l * points * pitch + t, points, stride=pitch), :] = total[:, 128 * l: 128 * l + 128]

    for chosen in (even, odd):
        for u in range(BATCH):
            chosen[pl.ds(u * depth + slots, depth - slots)] = jnp.zeros((depth - slots, 2, 128), jnp.float32)
    for u in range(BATCH):
        gather(u, u, even)

    def pair(h, _):
        first = 2 * BATCH * h
        for now, later in ((even, odd), (odd, even)):
            following = lax.min(first + BATCH, targets - BATCH)
            for u in range(BATCH):
                total = class_sums(first + u, u, now)
                gather(following + u, u, later)
                keep(first + u, total)
            first += BATCH
        return 0

    lax.fori_loop(0, targets // (2 * BATCH), pair, 0)

    for p in range(PARTS):
        fetch(p).wait()

    def multiply(i, total):
        left = jnp.concatenate(
            [sums[pl.ds((l * points + i) * pitch, targets), :].astype(jnp.bfloat16)
             for l in range(columns // 128)], axis=1)[:, :classes]
        return total + lax.dot_general(left, ops[i], (((1,), (1,)), ((), ())), preferred_element_type=jnp.float32)

    out_ref[...] = lax.fori_loop(0, points, multiply, jnp.zeros((targets, points), jnp.float32), unroll=4)


def translate(fine_mult, received, block_parents, entry_row, entry_class, entry_count, m2l_ops):
    targets, slots = entry_row.shape
    classes, points, _ = m2l_ops.shape
    depth = -(-slots // 64) * 64
    columns = -(-classes // 128) * 128
    total_rows = fine_mult.shape[0] + received.shape[0] * received.shape[1] * FOLD // (FOLD + 1)
    total_rows += block_parents.shape[0] * block_parents.shape[1] // 2
    live = lax.broadcasted_iota(jnp.int32, entry_row.shape, 1) < entry_count[:, None]
    kinds = jnp.pad(jnp.where(live, entry_class, -1), ((0, 0), (0, depth - slots)), constant_values=-1)
    smem = pl.BlockSpec(memory_space=pltpu.SMEM)
    vmem = pl.BlockSpec(memory_space=pltpu.VMEM)
    return pl.pallas_call(
        functools.partial(translate_kernel, targets, slots, classes, points),
        out_shape=jax.ShapeDtypeStruct((targets, points), jnp.float32),
        in_specs=[smem, vmem, vmem, vmem, vmem, pl.BlockSpec(memory_space=pl.ANY)],
        out_specs=vmem,
        scratch_shapes=[
            pltpu.VMEM((total_rows, 2, 128), jnp.float32),
            pltpu.VMEM((columns // 128 * points * (targets + EXTRA), 128), jnp.float32),
            pltpu.VMEM((points, points, classes), jnp.bfloat16),
            pltpu.VMEM((BATCH * depth, 2, 128), jnp.float32),
            pltpu.VMEM((BATCH * depth, 2, 128), jnp.float32),
            pltpu.SemaphoreType.DMA((PARTS,)),
        ],
        compiler_params=pltpu.CompilerParams(vmem_limit_bytes=62 * 2**20),
    )(entry_row.T.reshape(-1), kinds, fine_mult, received, block_parents, m2l_ops.transpose(1, 2, 0))


def body(
    fine_mult,
    m2m_ops,
    m2l_ops,
    check_to_equiv,
    l2l_ops,
    send_slots,
    fine_list,
    fine_class,
    fine_count,
    parent_list,
    parent_class,
    parent_count,
):
    cell_total, points = fine_mult.shape
    peer_count = send_slots.shape[1]
    capacity = send_slots.shape[2]
    subs = lax.axis_size("sub")
    rest = points - 128
    slots = send_slots[0].reshape(peer_count, FOLD, capacity // FOLD)
    cell = lax.broadcasted_iota(jnp.int32, (1, 1, cell_total), 2)
    onehot = (send_slots[0][:, :, None] == cell).astype(jnp.bfloat16).reshape(-1, cell_total)
    low = jnp.dot(onehot, fine_mult[:, :128], preferred_element_type=jnp.float32).astype(jnp.bfloat16)
    folded = jnp.concatenate([(slots[:, q, :, None] == cell).astype(jnp.bfloat16) for q in range(FOLD)], axis=2)
    placed = jnp.concatenate(
        [jnp.pad(fine_mult[:, 128:], ((0, 0), (rest * q, 128 - rest * (q + 1)))) for q in range(FOLD)], axis=0)
    high = jnp.dot(folded.reshape(-1, FOLD * cell_total), placed,
                   preferred_element_type=jnp.float32).astype(jnp.bfloat16)
    outgoing = jnp.concatenate(
        [low.reshape(peer_count, capacity, 128), high.reshape(peer_count, capacity // FOLD, 128)], axis=1)
    children = fine_mult.reshape(cell_total // 8, 8, points)
    parent_mult = jnp.einsum(
        "pkq,kqr->pr", children, m2m_ops, preferred_element_type=jnp.float32
    ).astype(jnp.bfloat16)
    mine = jnp.concatenate([parent_mult[:, :128], jnp.pad(parent_mult[:, 128:], ((0, 0), (0, 128 - rest)))], axis=0)
    received, block_parents = exchange(outgoing, mine, peer_count, subs)
    parent_first = cell_total + peer_count * capacity
    check = translate(
        fine_mult,
        received,
        block_parents,
        jnp.concatenate([fine_list, parent_list + parent_first], axis=0),
        jnp.concatenate([fine_class, parent_class], axis=0),
        jnp.concatenate([fine_count, parent_count], axis=0),
        m2l_ops,
    )
    fine_check, parent_check = check[:cell_total], 0.5 * check[cell_total:]
    parent_local = jnp.dot(
        parent_check,
        check_to_equiv,
        precision=lax.Precision.HIGHEST,
        preferred_element_type=jnp.float32,
    ).astype(jnp.bfloat16)
    downward = jnp.einsum("pq,kqr->pkr", parent_local, l2l_ops, preferred_element_type=jnp.float32)
    return fine_check + downward.reshape(cell_total, points)


def solution(mesh):
    in_specs = (
        P(("leaf", "sub"), None),
        P(),
        P(),
        P(),
        P(),
        P(("leaf", "sub"), None, None),
        P(("leaf", "sub"), None),
        P(("leaf", "sub"), None),
        P(("leaf", "sub")),
        P(("leaf", "sub"), None),
        P(("leaf", "sub"), None),
        P(("leaf", "sub")),
    )
    out_specs = P(("leaf", "sub"), None)
    return jax.shard_map(body, mesh=mesh, in_specs=in_specs, out_specs=out_specs, check_vma=False)
```

```python
import functools

import jax
import jax.numpy as jnp
from jax import lax
from jax.experimental import pallas as pl
from jax.experimental.pallas import tpu as pltpu
from jax.sharding import PartitionSpec as P

PARTS = 4
FOLD = 4
BATCH = 4
EXTRA = 1


def exchange_kernel(peers, subs, out_ref, mine_ref, received_ref, parents_ref, send_sems, recv_sems, parent_send,
                    parent_recv, own_sems):
    leaf, sub = lax.axis_index("leaf"), lax.axis_index("sub")
    me = leaf * subs + sub
    barrier = pltpu.get_barrier_semaphore()

    def cells(o):
        other = lax.rem(me + o, peers)
        return pltpu.make_async_remote_copy(
            src_ref=out_ref.at[other], dst_ref=received_ref.at[me], send_sem=send_sems.at[o], recv_sem=recv_sems.at[o],
            device_id=(other // subs, lax.rem(other, subs)), device_id_type=pl.DeviceIdType.MESH)

    def parents(o):
        return pltpu.make_async_remote_copy(
            src_ref=mine_ref, dst_ref=parents_ref.at[sub], send_sem=parent_send.at[o], recv_sem=parent_recv.at[o],
            device_id=(leaf, lax.rem(sub + o, subs)), device_id_type=pl.DeviceIdType.MESH)

    def greet(o, _):
        other = lax.rem(me + o, peers)
        pl.semaphore_signal(barrier, inc=1, device_id=(other // subs, lax.rem(other, subs)),
                            device_id_type=pl.DeviceIdType.MESH)
        return 0

    lax.fori_loop(1, peers, greet, 0)
    own = pltpu.make_async_copy(out_ref.at[me], received_ref.at[me], own_sems.at[0])
    own_parents = pltpu.make_async_copy(mine_ref, parents_ref.at[sub], own_sems.at[1])
    own.start()
    own_parents.start()
    pl.semaphore_wait(barrier, peers - 1)

    def start(o, _):
        cells(o).start()
        return 0

    def finish(o, _):
        cells(o).wait()
        return 0

    lax.fori_loop(1, peers, start, 0)
    for o in range(1, subs):
        parents(o).start()
    own.wait()
    own_parents.wait()
    for o in range(1, subs):
        parents(o).wait()
    lax.fori_loop(1, peers, finish, 0)


def exchange(outgoing, mine, peers, subs):
    vmem = pl.BlockSpec(memory_space=pltpu.VMEM)
    return pl.pallas_call(
        functools.partial(exchange_kernel, peers, subs),
        out_shape=(jax.ShapeDtypeStruct(outgoing.shape, outgoing.dtype),
                   jax.ShapeDtypeStruct((subs,) + mine.shape, mine.dtype)),
        in_specs=[vmem, vmem],
        out_specs=(vmem, vmem),
        scratch_shapes=[
            pltpu.SemaphoreType.DMA((peers,)),
            pltpu.SemaphoreType.DMA((peers,)),
            pltpu.SemaphoreType.DMA((subs,)),
            pltpu.SemaphoreType.DMA((subs,)),
            pltpu.SemaphoreType.DMA((2,)),
        ],
        compiler_params=pltpu.CompilerParams(collective_id=0, has_side_effects=True, vmem_limit_bytes=16 * 2**20),
    )(outgoing, mine)


def translate_kernel(targets, slots, classes, points, row_ref, kind_ref, mult_ref, received_ref, parents_ref, ops_ref,
                     out_ref, table_ref, sums, ops, even, odd, sems):
    part = points // PARTS
    columns = -(-classes // 128) * 128
    depth = even.shape[0] // BATCH
    pitch = targets + EXTRA

    def fetch(p):
        piece = pl.ds(p * part, part)
        return pltpu.make_async_copy(ops_ref.at[piece], ops.at[piece], sems.at[p])

    for p in range(PARTS):
        fetch(p).start()

    cells = mult_ref.shape[0]
    peers, packed, _ = received_ref.shape
    subs, both, _ = parents_ref.shape
    capacity, own = packed * FOLD // (FOLD + 1), both // 2
    rest = points - 128
    rows = table_ref.reshape(table_ref.shape[0] * 2, 128)
    mult = mult_ref[...].astype(jnp.float32)
    rows[pl.ds(0, cells, stride=2), :] = mult[:, :128]
    rows[pl.ds(1, cells, stride=2), :] = jnp.concatenate(
        [mult[:, 128:], jnp.zeros((cells, 128 - rest), jnp.float32)], axis=1)

    def unpack(s, _):
        first = 2 * (cells + s * capacity)
        rows[pl.ds(first, capacity, stride=2), :] = received_ref[s, :capacity].astype(jnp.float32)
        high = received_ref[s, capacity:].astype(jnp.float32)
        for q in range(FOLD):
            rows[pl.ds(first + 2 * q * (capacity // FOLD) + 1, capacity // FOLD, stride=2), :] = (
                pltpu.roll(high, 128 - rest * q, 1) if q else high)
        return 0

    lax.fori_loop(0, peers, unpack, 0)
    for s in range(subs):
        first = 2 * (cells + peers * capacity + s * own)
        rows[pl.ds(first, own, stride=2), :] = parents_ref[s, :own].astype(jnp.float32)
        rows[pl.ds(first + 1, own, stride=2), :] = parents_ref[s, own:].astype(jnp.float32)

    def gather(t, u, chosen):
        for e in range(slots):
            place = 2 * (u * depth + e)
            chosen.reshape(2 * BATCH * depth, 128)[place: place + 2, :] = (
                rows[pl.ds(pl.multiple_of(row_ref[e * targets + t], 2), 2), :])

    def class_sums(t, u, chosen):
        flat = chosen.reshape(2 * BATCH * depth, 128)
        low = flat[pl.ds(2 * u * depth, depth, stride=2), :].astype(jnp.bfloat16)
        high = flat[pl.ds(2 * u * depth + 1, depth, stride=2), :].astype(jnp.bfloat16)
        left = jnp.concatenate([low, high], axis=1)[:, :points].T
        kinds = kind_ref[pl.ds(t, 1), :]
        wanted = lax.broadcasted_iota(jnp.int32, (columns, depth), 0)
        onehot = jnp.where(kinds == wanted, 1.0, 0.0).astype(jnp.bfloat16)
        return lax.dot_general(left, onehot, (((1,), (1,)), ((), ())), preferred_element_type=jnp.float32)

    def keep(t, total):
        for l in range(columns // 128):
            sums[pl.ds(l * points * pitch + t, points, stride=pitch), :] = total[:, 128 * l: 128 * l + 128]

    for chosen in (even, odd):
        for u in range(BATCH):
            chosen[pl.ds(u * depth + slots, depth - slots)] = jnp.zeros((depth - slots, 2, 128), jnp.float32)
    for u in range(BATCH):
        gather(u, u, even)

    def pair(h, _):
        first = 2 * BATCH * h
        for now, later in ((even, odd), (odd, even)):
            following = lax.min(first + BATCH, targets - BATCH)
            for u in range(BATCH):
                total = class_sums(first + u, u, now)
                gather(following + u, u, later)
                keep(first + u, total)
            first += BATCH
        return 0

    lax.fori_loop(0, targets // (2 * BATCH), pair, 0)

    for p in range(PARTS):
        fetch(p).wait()

    def multiply(i, total):
        left = jnp.concatenate(
            [sums[pl.ds((l * points + i) * pitch, targets), :].astype(jnp.bfloat16)
             for l in range(columns // 128)], axis=1)[:, :classes]
        return total + lax.dot_general(left, ops[i], (((1,), (1,)), ((), ())), preferred_element_type=jnp.float32)

    out_ref[...] = lax.fori_loop(0, points, multiply, jnp.zeros((targets, points), jnp.float32), unroll=8)


def translate(fine_mult, received, block_parents, entry_row, entry_class, entry_count, m2l_ops):
    targets, slots = entry_row.shape
    classes, points, _ = m2l_ops.shape
    depth = -(-slots // 64) * 64
    columns = -(-classes // 128) * 128
    total_rows = fine_mult.shape[0] + received.shape[0] * received.shape[1] * FOLD // (FOLD + 1)
    total_rows += block_parents.shape[0] * block_parents.shape[1] // 2
    live = lax.broadcasted_iota(jnp.int32, entry_row.shape, 1) < entry_count[:, None]
    kinds = jnp.pad(jnp.where(live, entry_class, -1), ((0, 0), (0, depth - slots)), constant_values=-1)
    smem = pl.BlockSpec(memory_space=pltpu.SMEM)
    vmem = pl.BlockSpec(memory_space=pltpu.VMEM)
    return pl.pallas_call(
        functools.partial(translate_kernel, targets, slots, classes, points),
        out_shape=jax.ShapeDtypeStruct((targets, points), jnp.float32),
        in_specs=[smem, vmem, vmem, vmem, vmem, pl.BlockSpec(memory_space=pl.ANY)],
        out_specs=vmem,
        scratch_shapes=[
            pltpu.VMEM((total_rows, 2, 128), jnp.float32),
            pltpu.VMEM((columns // 128 * points * (targets + EXTRA), 128), jnp.float32),
            pltpu.VMEM((points, points, classes), jnp.bfloat16),
            pltpu.VMEM((BATCH * depth, 2, 128), jnp.float32),
            pltpu.VMEM((BATCH * depth, 2, 128), jnp.float32),
            pltpu.SemaphoreType.DMA((PARTS,)),
        ],
        compiler_params=pltpu.CompilerParams(vmem_limit_bytes=62 * 2**20),
    )(2 * entry_row.T.reshape(-1), kinds, fine_mult, received, block_parents, m2l_ops.transpose(1, 2, 0))


def body(
    fine_mult,
    m2m_ops,
    m2l_ops,
    check_to_equiv,
    l2l_ops,
    send_slots,
    fine_list,
    fine_class,
    fine_count,
    parent_list,
    parent_class,
    parent_count,
):
    cell_total, points = fine_mult.shape
    peer_count = send_slots.shape[1]
    capacity = send_slots.shape[2]
    subs = lax.axis_size("sub")
    rest = points - 128
    slots = send_slots[0].reshape(peer_count, FOLD, capacity // FOLD)
    cell = lax.broadcasted_iota(jnp.int32, (1, 1, cell_total), 2)
    onehot = (send_slots[0][:, :, None] == cell).astype(jnp.bfloat16).reshape(-1, cell_total)
    low = jnp.dot(onehot, fine_mult[:, :128], preferred_element_type=jnp.float32).astype(jnp.bfloat16)
    folded = jnp.concatenate([(slots[:, q, :, None] == cell).astype(jnp.bfloat16) for q in range(FOLD)], axis=2)
    placed = jnp.concatenate(
        [jnp.pad(fine_mult[:, 128:], ((0, 0), (rest * q, 128 - rest * (q + 1)))) for q in range(FOLD)], axis=0)
    high = jnp.dot(folded.reshape(-1, FOLD * cell_total), placed,
                   preferred_element_type=jnp.float32).astype(jnp.bfloat16)
    outgoing = jnp.concatenate(
        [low.reshape(peer_count, capacity, 128), high.reshape(peer_count, capacity // FOLD, 128)], axis=1)
    children = fine_mult.reshape(cell_total // 8, 8, points)
    parent_mult = jnp.einsum(
        "pkq,kqr->pr", children, m2m_ops, preferred_element_type=jnp.float32
    ).astype(jnp.bfloat16)
    mine = jnp.concatenate([parent_mult[:, :128], jnp.pad(parent_mult[:, 128:], ((0, 0), (0, 128 - rest)))], axis=0)
    received, block_parents = exchange(outgoing, mine, peer_count, subs)
    parent_first = cell_total + peer_count * capacity
    check = translate(
        fine_mult,
        received,
        block_parents,
        jnp.concatenate([fine_list, parent_list + parent_first], axis=0),
        jnp.concatenate([fine_class, parent_class], axis=0),
        jnp.concatenate([fine_count, parent_count], axis=0),
        m2l_ops,
    )
    fine_check, parent_check = check[:cell_total], 0.5 * check[cell_total:]
    parent_local = jnp.dot(
        parent_check,
        check_to_equiv,
        precision=lax.Precision.HIGHEST,
        preferred_element_type=jnp.float32,
    ).astype(jnp.bfloat16)
    downward = jnp.einsum("pq,kqr->pkr", parent_local, l2l_ops, preferred_element_type=jnp.float32)
    return fine_check + downward.reshape(cell_total, points)


def solution(mesh):
    in_specs = (
        P(("leaf", "sub"), None),
        P(),
        P(),
        P(),
        P(),
        P(("leaf", "sub"), None, None),
        P(("leaf", "sub"), None),
        P(("leaf", "sub"), None),
        P(("leaf", "sub")),
        P(("leaf", "sub"), None),
        P(("leaf", "sub"), None),
        P(("leaf", "sub")),
    )
    out_specs = P(("leaf", "sub"), None)
    return jax.shard_map(body, mesh=mesh, in_specs=in_specs, out_specs=out_specs, check_vma=False)
```
